32 devices in a mesh: gx: 4 (over y, x), gy: 2 (over core), gz: 4 (over z).
Axes of the slice: x: 2, y: 2, z: 4, core: 2. Of those that a mesh axis runs over, the one named last changes fastest.
Arguments:
- local_schur: bfloat16 [4, 2, 4, 882, 882], P('gx', 'gy', 'gz'), may hold values from -15 to 20, as said below
- schur_inverse: bfloat16 [4, 2, 4, 882, 882], P('gx', 'gy', 'gz'), may hold values from -1.5 to 2, as said below
- load_terms: bfloat16 [4, 2, 4, 6, 147, 128], P('gx', 'gy', 'gz'), may hold values from -6 to 6
- corner_basis: float32 [4, 2, 4, 8, 882], P('gx', 'gy', 'gz'), may hold values from -0.21875 to 0.21875
- corner_map: int32 [4, 2, 4, 8], replicated, may hold values from 0 to 9, as said below
- coarse_inverse: bfloat16 [9, 9], replicated, may hold values from -6 to 8, as said below
Outputs:
- solution: float32 [4, 2, 4, 6, 147, 128], P('gx', 'gy', 'gz')
The draws below stay inside these ranges and needn't reach their ends.
Inputs may be any that keep to these rules, and one draw needn't show every extreme that they name: `local_schur`: each 882 x 882 matrix is symmetric positive definite. `schur_inverse`: each 882 x 882 matrix is symmetric positive definite. `coarse_inverse`: symmetric positive definite. `corner_map`: corner k of subdomain (a, b, c) is the lattice point (a + k // 4, b + (k // 2) % 2, c + k % 2) of the (5) x (3) x (5) corner lattice; points on the lattice's outside have the number 9, interior points are numbered 0 to 8 by a permutation, so subdomains that meet at a point give it the same number.
All inputs are finite; a program needn't handle non-finite values.
Results may differ from the reference program's by a relative error of at most 0.0022.
Values may be sent and summed in bfloat16 or wider, within the bound.
A program may use at most 64 MiB of HBM per device.

```python
import math
import jax
import jax.numpy as jnp
from jax import lax

F = 147
FACES = 6
CORNERS = 8
NRHS = 128
ITERS = 3
IFACE = 882
SX = 4
SY = 2
SZ = 4
NCORNER = 9


def spd_matrices(key, leading, order, lowest, highest):
    count = 1
    for extent in leading:
        count = count * extent

    def one_matrix(index):
        sub_key = jax.random.fold_in(key, index)
        key_diag, key_off = jax.random.split(sub_key, 2)
        diagonal = jnp.exp(jax.random.uniform(key_diag, (order,), dtype=jnp.float32, minval=math.log(lowest), maxval=math.log(highest)))
        mixed = jax.random.uniform(key_off, (order, order), dtype=jnp.float32, minval=-1.0, maxval=1.0)
        factor = math.sqrt(3.0) * mixed
        gram = jnp.dot(factor, factor.T, precision=lax.Precision.HIGHEST) / order
        gram = 0.5 * (gram + gram.T)
        core = 0.5 * (jnp.eye(order, dtype=jnp.float32) + gram)
        root = jnp.sqrt(diagonal)
        return root[:, None] * core * root[None, :]
    stacked = lax.map(one_matrix, jnp.arange(count, dtype=jnp.int32))
    return stacked.reshape(leading + (order, order))


def schur_matrices(key, leading, order, lowest, highest):
    count = 1
    for extent in leading:
        count = count * extent
    rank_cols = max(4, order * 4 // 55)

    def one_matrix(index):
        sub_key = jax.random.fold_in(key, index)
        key_diag = jax.random.fold_in(sub_key, 0)
        key_low = jax.random.fold_in(sub_key, 1)
        key_weight = jax.random.fold_in(sub_key, 3)
        key_full = jax.random.fold_in(sub_key, 4)
        weights = jnp.exp(jax.random.uniform(key_weight, (rank_cols,), dtype=jnp.float32, minval=math.log(0.02), maxval=0.0))
        diagonal = jnp.exp(jax.random.uniform(key_diag, (order,), dtype=jnp.float32, minval=math.log(lowest), maxval=math.log(highest)))
        factor = jax.random.uniform(key_low, (order, rank_cols), dtype=jnp.float32, minval=-1.0, maxval=1.0)
        weighted = factor * jnp.sqrt(weights)[None, :]
        low_part = jnp.dot(weighted, weighted.T, precision=lax.Precision.HIGHEST) * (8.0 / rank_cols)
        full_factor = math.sqrt(3.0) * jax.random.uniform(key_full, (order, order), dtype=jnp.float32, minval=-1.0, maxval=1.0)
        full_part = jnp.dot(full_factor, full_factor.T, precision=lax.Precision.HIGHEST) / order
        core = 0.025 * (jnp.eye(order, dtype=jnp.float32) + 0.25 * full_part) + low_part
        core = 0.5 * (core + core.T)
        root = jnp.sqrt(diagonal)
        return root[:, None] * core * root[None, :]
    stacked = lax.map(one_matrix, jnp.arange(count, dtype=jnp.int32))
    return stacked.reshape(leading + (order, order))


def draw_local_schur(key, part):
    return schur_matrices(jax.random.fold_in(key, 11), (SX, SY, SZ), IFACE, 1.0, 10.0).astype(jnp.bfloat16)


def draw_schur_inverse(key, part):
    return spd_matrices(jax.random.fold_in(key, 12), (SX, SY, SZ), IFACE, 0.1, 1.0).astype(jnp.bfloat16)


def draw_coarse_inverse(key, part):
    return spd_matrices(jax.random.fold_in(key, 13), (), NCORNER, 1.0, 4.0).astype(jnp.bfloat16)


def draw_corner_map(key, part):
    along_x = jnp.arange(SX, dtype=jnp.int32)[:, None, None, None]
    along_y = jnp.arange(SY, dtype=jnp.int32)[None, :, None, None]
    along_z = jnp.arange(SZ, dtype=jnp.int32)[None, None, :, None]
    corner_ids = jnp.arange(8, dtype=jnp.int32)[None, None, None, :]
    point_x = along_x + corner_ids // 4
    point_y = along_y + corner_ids // 2 % 2
    point_z = along_z + corner_ids % 2
    inside = (point_x >= 1) & (point_x <= SX - 1) & (point_y >= 1) & (point_y <= SY - 1) & (point_z >= 1) & (point_z <= SZ - 1)
    interior = ((point_x - 1) * (SY - 1) + (point_y - 1)) * (SZ - 1) + (point_z - 1)
    interior = jnp.where(inside, interior, 0).astype(jnp.int32)
    numbering = jax.random.permutation(jax.random.fold_in(key, 14), NCORNER).astype(jnp.int32)
    return jnp.where(inside, numbering[interior], NCORNER).astype(jnp.int32)


def block_levels(key, dims, shards, low, high):
    def one(axis_at, shards_of):
        draws = jax.random.uniform(jax.random.fold_in(jax.random.fold_in(key, 6), axis_at), (shards_of,), jnp.float32, low / len(shards), high / len(shards))
        return jnp.repeat(jnp.exp(draws), dims[axis_at] // shards_of).reshape((-1,) + (1,) * (len(dims) - axis_at - 1))

    factor_of = one(*shards[0])
    for cut in shards[1:]:
        factor_of = factor_of * one(*cut)
    return factor_of


def bell_draw(rng, shape, scale, bound, cuts=(), held_as=jnp.bfloat16):
    values = scale * jax.random.normal(rng, shape, jnp.float32)
    if cuts:
        values = values * block_levels(rng, shape, cuts, -0.22, 0.18)
    return jnp.clip(values, -bound, bound).astype(held_as)


def setup_inputs(seed: int = 0) -> dict:
    splits = jax.random.split(jax.random.key(seed), 7)
    local_schur = draw_local_schur(jax.random.fold_in(splits[6], 71), 0)
    schur_inverse = draw_schur_inverse(jax.random.fold_in(splits[6], 71), 0)
    load_terms = bell_draw(splits[2], (SX, SY, SZ, FACES, F, NRHS), 1.0, 6.0, ((0, 4), (1, 2), (2, 4)))
    corner_basis = bell_draw(splits[3], (SX, SY, SZ, CORNERS, IFACE), IFACE ** -0.5, 0.21875, ((0, 4), (1, 2), (2, 4)), jnp.float32)
    corner_map = draw_corner_map(jax.random.fold_in(splits[6], 71), 0)
    coarse_inverse = draw_coarse_inverse(jax.random.fold_in(splits[6], 71), 0)
    return {"local_schur": local_schur, "schur_inverse": schur_inverse, "load_terms": load_terms, "corner_basis": corner_basis, "corner_map": corner_map, "coarse_inverse": coarse_inverse}


def move_down(values, axis):
    zero_rim = jnp.zeros_like(lax.slice_in_dim(values, 0, 1, axis=axis))
    kept = lax.slice_in_dim(values, 0, values.shape[axis] - 1, axis=axis)
    return jnp.concatenate([zero_rim, kept], axis=axis)

def move_up(values, axis):
    zero_rim = jnp.zeros_like(lax.slice_in_dim(values, 0, 1, axis=axis))
    kept = lax.slice_in_dim(values, 1, values.shape[axis], axis=axis)
    return jnp.concatenate([kept, zero_rim], axis=axis)

def neighbour_faces(array):
    pieces = []
    for axis in range(3):
        minus_face = array[:, :, :, 2 * axis]
        plus_face = array[:, :, :, 2 * axis + 1]
        pieces.append(move_down(plus_face, axis))
        pieces.append(move_up(minus_face, axis))
    return jnp.stack(pieces, axis=3)

def face_mask():
    extents = (SX, SY, SZ)
    columns = []
    for axis in range(3):
        position = lax.broadcasted_iota(jnp.int32, (SX, SY, SZ), axis)
        columns.append(position > 0)
        columns.append(position < extents[axis] - 1)
    return jnp.stack(columns, axis=3).astype(jnp.float32)

def deluxe_of(blocks_wide, pair_sum):
    lower_factor = jnp.linalg.cholesky(pair_sum)
    half_solve = lax.linalg.triangular_solve(lower_factor, blocks_wide, left_side=True, lower=True)
    return lax.linalg.triangular_solve(lower_factor, half_solve, left_side=True, lower=True, transpose_a=True)

def apply_local(matrices, vectors):

    def one_slab(operands):
        return jnp.einsum('yzab,yzbn->yzan', operands[0].astype(jnp.float32), operands[1].astype(jnp.float32), precision=lax.Precision.HIGHEST)
    return lax.map(one_slab, (matrices, vectors))

def reference(local_schur, schur_inverse, load_terms, corner_basis, corner_map, coarse_inverse):
    highest = lax.Precision.HIGHEST
    live_faces = face_mask()[:, :, :, :, None, None]

    def assemble(values):
        return (values + neighbour_faces(values)) * live_faces
    shaped = local_schur.reshape(SX, SY, SZ, FACES, F, FACES, F)
    blocks = jnp.stack([shaped[:, :, :, f, :, f, :] for f in range(FACES)], axis=3).astype(jnp.float32)
    deluxe = deluxe_of(blocks, blocks + neighbour_faces(blocks))

    def inner_product(left, right):
        return 0.5 * jnp.sum(left * right, axis=(0, 1, 2, 3, 4))

    def precondition(residual):
        scaled = jnp.einsum('xyzfab,xyzfan->xyzfbn', deluxe, residual, precision=highest)
        flat_scaled = scaled.reshape(SX, SY, SZ, IFACE, NRHS)
        corner_part = jnp.einsum('xyzka,xyzan->xyzkn', corner_basis, flat_scaled, precision=highest)
        coarse_res = jax.ops.segment_sum(corner_part.reshape(-1, NRHS), corner_map.reshape(-1), num_segments=NCORNER + 1)[:NCORNER]
        coarse_value = jnp.dot(coarse_inverse.astype(jnp.float32), coarse_res.astype(jnp.bfloat16).astype(jnp.float32), preferred_element_type=jnp.float32)
        padded_value = jnp.concatenate([coarse_value, jnp.zeros((1, NRHS), jnp.float32)], axis=0)
        picked = padded_value[corner_map]
        local_value = apply_local(schur_inverse, flat_scaled.astype(jnp.bfloat16))
        local_value = local_value + jnp.einsum('xyzka,xyzkn->xyzan', corner_basis, picked, precision=highest)
        local_faces = local_value.reshape(SX, SY, SZ, FACES, F, NRHS)
        return assemble(jnp.einsum('xyzfab,xyzfbn->xyzfan', deluxe, local_faces, precision=highest))

    def image_of(direction):
        product = apply_local(local_schur, direction.reshape(SX, SY, SZ, IFACE, NRHS).astype(jnp.bfloat16))
        return assemble(product.reshape(SX, SY, SZ, FACES, F, NRHS))
    load = assemble(load_terms.astype(jnp.float32))
    solution = jnp.zeros_like(load)
    residual = load
    precond_res = precondition(residual)
    direction = precond_res
    rho_now = inner_product(residual, precond_res)
    for iteration in range(ITERS):
        image_field = image_of(direction)
        step_size = rho_now / inner_product(direction, image_field)
        solution = solution + step_size * direction
        residual = residual - step_size * image_field
        if iteration + 1 < ITERS:
            precond_res = precondition(residual)
            rho_next = inner_product(residual, precond_res)
            direction = precond_res + rho_next / rho_now * direction
            rho_now = rho_next
    return solution
```

```python
import functools
import math

import jax
import jax.numpy as jnp
from jax import lax
from jax.experimental import pallas as pl
from jax.experimental.pallas import tpu as pltpu
from jax.sharding import PartitionSpec as P

ITERS = 3
FACES = 6
AXES = ("gx", "gy", "gz")
PANEL = 8
VMEM_BYTES = 50 * 1024 * 1024
HIGHEST = lax.Precision.HIGHEST
MESH = pl.DeviceIdType.MESH


def dot(left, right, dims=((1,), (0,)), precision=None):
    return lax.dot_general(
        left, right, (dims, ((), ())), precision=precision, preferred_element_type=jnp.float32
    )


def split2(values):
    high = values.astype(jnp.bfloat16)
    low = (values - high.astype(jnp.float32)).astype(jnp.bfloat16)
    return high, low


def split3(values):
    first = values.astype(jnp.bfloat16).astype(jnp.float32)
    rest = values - first
    second = rest.astype(jnp.bfloat16).astype(jnp.float32)
    return first, second, rest - second


def group_index(group):
    index = 0
    for axis in group:
        index = index * lax.axis_size(axis) + lax.axis_index(axis)
    return index


def group_size(group):
    return math.prod(lax.axis_size(axis) for axis in group)


def group_device(group, index):
    where = {}
    for axis in reversed(group):
        size = lax.axis_size(axis)
        where[axis] = index % size
        index = index // size
    return where


def live_face(face):
    axis = AXES[face // 2]
    place = lax.axis_index(axis)
    return place < lax.axis_size(axis) - 1 if face % 2 else place > 0


def across(face):
    axis = AXES[face // 2]
    return {axis: lax.axis_index(axis) + (1 if face % 2 else -1)}


def face_copy(face, source, target, send_sems, recv_sems):
    return pltpu.make_async_remote_copy(
        src_ref=source.at[face],
        dst_ref=target.at[face ^ 1],
        send_sem=send_sems.at[face],
        recv_sem=recv_sems.at[face ^ 1],
        device_id=across(face),
        device_id_type=MESH,
    )


def send_face(face, *refs):
    @pl.when(live_face(face))
    def _():
        face_copy(face, *refs).start()


def wait_face(face, source, target, send_sems, recv_sems):
    @pl.when(live_face(face))
    def _():
        copy = pltpu.make_async_remote_copy(
            src_ref=source.at[face],
            dst_ref=target.at[face],
            send_sem=send_sems.at[face],
            recv_sem=recv_sems.at[face],
            device_id=across(face),
            device_id_type=MESH,
        )
        copy.wait_recv()
        copy.wait_send()


def exchange_kernel(blocks, load, near_blocks, near_load, block_send, block_recv, load_send, load_recv):
    barrier = pltpu.get_barrier_semaphore()
    for face in range(FACES):
        @pl.when(live_face(face))
        def _():
            pl.semaphore_signal(barrier, inc=1, device_id=across(face), device_id_type=MESH)
    pl.semaphore_wait(barrier, sum(live_face(face).astype(jnp.int32) for face in range(FACES)))
    for face in range(FACES):
        send_face(face, blocks, near_blocks, block_send, block_recv)
    for face in range(FACES):
        send_face(face, load, near_load, load_send, load_recv)
    for face in range(FACES):
        wait_face(face, blocks, near_blocks, block_send, block_recv)
    for face in range(FACES):
        wait_face(face, load, near_load, load_send, load_recv)


def inverse_kernel(size, live, blocks, near, basis, hot, d_high, d_low, t_high, t_low, gather, work):
    padded = work.shape[1]
    rows = lax.broadcasted_iota(jnp.int32, (padded, padded), 0)
    cols = lax.broadcasted_iota(jnp.int32, (padded, padded), 1)
    unit = jnp.where((rows == cols) & (rows >= size), 1.0, 0.0)
    for face in range(FACES):
        block = blocks[face].astype(jnp.float32)[:padded, :padded]
        other = near[face].astype(jnp.float32)[:padded, :padded]
        block = block + jnp.where(live[face] > 0, other, 0.0)
        work[face] = jnp.where((rows < size) & (cols < size), block, unit)
    lane = lax.broadcasted_iota(jnp.int32, (PANEL, padded), 1)
    row = lax.broadcasted_iota(jnp.int32, (PANEL, padded), 0)
    for start in range(0, padded, PANEL):
        panels = [work[face, start : start + PANEL, :] for face in range(FACES)]
        swept = list(panels)
        for step in range(0, PANEL, 2):
            pivot = start + step
            first, second = lane[:1] == pivot, lane[:1] == pivot + 1
            both = (lane == pivot) | (lane == pivot + 1)
            for face in range(FACES):
                held = swept[face]
                left = jnp.broadcast_to(held[:, pivot : pivot + 1], held.shape)
                right = jnp.broadcast_to(held[:, pivot + 1 : pivot + 2], held.shape)
                a, b = left[step : step + 1], left[step + 1 : step + 2]
                c = right[step + 1 : step + 2]
                scale = 1.0 / (a * c - b * b)
                upper = jnp.where(both[:1], jnp.where(first, 1.0, 0.0), held[step : step + 1])
                lower = jnp.where(both[:1], jnp.where(second, 1.0, 0.0), held[step + 1 : step + 2])
                upper, lower = (c * upper - b * lower) * scale, (a * lower - b * upper) * scale
                kept = jnp.where(both, 0.0, held) - left * upper - right * lower
                swept[face] = jnp.where(row == step, upper, jnp.where(row == step + 1, lower, kept))
        inside = (lane >= start) & (lane < start + PANEL)
        column_inside = (cols >= start) & (cols < start + PANEL)
        for face in range(FACES):
            signed = jnp.where(inside, -swept[face], swept[face])
            u0, u1, u2 = split3(panels[face])
            w0, w1, w2 = split3(signed)
            left = jnp.concatenate([u0, u0, u1, u1, u0, u2], axis=0).astype(jnp.bfloat16)
            right = jnp.concatenate([w0, w1, w0, w1, w2, w0], axis=0).astype(jnp.bfloat16)
            change = dot(left, right, ((0,), (0,)))
            work[face] = jnp.where(column_inside, 0.0, work[face]) - change
            work[face, start : start + PANEL, :] = signed
    for face in range(FACES):
        inverse = -work[face][:size, :size]
        block = blocks[face].astype(jnp.float32)[:size, :size].astype(jnp.bfloat16)
        parts = [part.astype(jnp.bfloat16) for part in split3(inverse)]
        deluxe = dot(parts[0], block) + (dot(parts[1], block) + dot(parts[2], block))
        turned = dot(block, parts[0]) + (dot(block, parts[1]) + dot(block, parts[2]))
        d_high[face], d_low[face] = split2(deluxe)
        corner = dot(hot[...], basis[face], precision=HIGHEST)
        rows_up = dot(corner, turned, precision=HIGHEST)
        gather[face] = rows_up
        top = rows_up.shape[0]
        t_high[face, :top], t_low[face, :top] = split2(rows_up)
        t_high[face, top:], t_low[face, top:] = split2(turned)


def cg_kernel(
    groups, schur, inverse, load, near_load, d_high, d_low, t_high, t_low, gather, coarse, out,
    near_gather, own, near, wide_own, wide_near, residual, direction, flat, wide_sums, thin_sums,
    halo_send, halo_recv, gather_send, gather_recv, sum_send, sum_recv,
):
    size = load.shape[1]
    cases = load.shape[2]
    sizes = [group_size(group) for group in groups]
    bases = [sum(sizes[:stage]) for stage in range(len(groups))]
    places = [group_index(group) for group in groups]
    live = [live_face(face) for face in range(FACES)]

    barrier = pltpu.get_barrier_semaphore()
    for stage, group in enumerate(groups):
        for away in range(1, sizes[stage]):
            peer = (places[stage] + away) % sizes[stage]
            pl.semaphore_signal(barrier, inc=1, device_id=group_device(group, peer), device_id_type=MESH)
    pl.semaphore_wait(barrier, sum(sizes) - len(groups))

    def part_copy(sums, call, stage, slot, peer, sem_slot):
        place = bases[stage] + slot
        return pltpu.make_async_remote_copy(
            src_ref=sums.at[place],
            dst_ref=sums.at[place],
            send_sem=sum_send.at[call, bases[stage] + peer],
            recv_sem=sum_recv.at[call, bases[stage] + sem_slot],
            device_id=group_device(groups[stage], peer),
            device_id_type=MESH,
        )

    def start_sum(sums, call, stage, value):
        me = places[stage]
        sums[bases[stage] + me] = value
        for away in range(1, sizes[stage]):
            peer = (me + away) % sizes[stage]
            part_copy(sums, call, stage, me, peer, me).start()

    def end_sum(sums, call, stage):
        me = places[stage]
        for away in range(1, sizes[stage]):
            peer = (me + away) % sizes[stage]
            part_copy(sums, call, stage, peer, peer, peer).wait_recv()
        total = sums[bases[stage]]
        for slot in range(1, sizes[stage]):
            total = total + sums[bases[stage] + slot]
        return total

    def finish_sum(sums, call):
        total = end_sum(sums, call, 0)
        for stage in range(1, len(groups)):
            start_sum(sums, call, stage, total)
            total = end_sum(sums, call, stage)
        return total

    def drain_sum(sums, call):
        for stage in range(len(groups)):
            me = places[stage]
            for away in range(1, sizes[stage]):
                peer = (me + away) % sizes[stage]
                part_copy(sums, call, stage, me, peer, me).wait_send()

    def rows_of(face):
        return slice(face * size, (face + 1) * size)

    for face in range(FACES):
        send_face(face, gather, near_gather, gather_send, gather_recv)
    for face in range(FACES):
        total = load[face].astype(jnp.float32) + near_load[face].astype(jnp.float32)
        residual[face] = jnp.where(live[face], total, 0.0)

    wide_rows = wide_sums.shape[2]
    last_row = lax.broadcasted_iota(jnp.int32, (wide_rows, cases), 0) == wide_rows - 1

    for turn in range(ITERS):
        wide = wide_sums.at[turn]
        corner_part = jnp.zeros((wide_rows, cases), jnp.float32)
        for face in range(FACES):
            held = residual[face]
            high, low = split2(held)
            both = dot(t_high[face], high) + (dot(t_low[face], high) + dot(t_high[face], low))
            corner_part = corner_part + both[:wide_rows]
            flat[rows_of(face), :] = both[wide_rows:]
        scaled = flat[...]
        local_value = dot(inverse[...], scaled.astype(jnp.bfloat16))
        rho_part = jnp.sum(scaled * local_value, axis=0, keepdims=True)
        start_sum(wide, 2 * turn, 0, corner_part + jnp.where(last_row, rho_part, 0.0))
        flat[...] = local_value
        halo = (own.at[turn], near.at[turn], halo_send.at[2 * turn], halo_recv.at[2 * turn])
        for face in range(FACES):
            high, low = split2(flat[rows_of(face), :])
            value = dot(d_high[face], high) + (dot(d_low[face], high) + dot(d_high[face], low))
            own[turn, face] = value
            send_face(face, *halo)
        total = finish_sum(wide, 2 * turn)
        coarse_value = dot(coarse[...], total.astype(jnp.bfloat16))
        rho_next = jnp.sum(jnp.where(last_row, total, total * coarse_value), axis=0, keepdims=True)
        value_high, value_low = split2(coarse_value)
        if turn == 0:
            for face in range(FACES):
                wait_face(face, gather, near_gather, gather_send, gather_recv)
        for face in range(FACES):
            wait_face(face, *halo)
            high, low = split2(gather[face] + near_gather[face])
            step_z = own[turn, face] + near[turn, face] + dot(high, value_high, ((0,), (0,)))
            step_z = step_z + (dot(low, value_high, ((0,), (0,))) + dot(high, value_low, ((0,), (0,))))
            if turn > 0:
                step_z = step_z + rho_next / rho * direction[face]
            step_z = jnp.where(live[face], step_z, 0.0)
            direction[face] = step_z
            flat[rows_of(face), :] = step_z
        rho = rho_next
        thin = thin_sums.at[turn]
        wide_direction = flat[...]
        image = dot(schur[...], wide_direction.astype(jnp.bfloat16))
        bend = jnp.sum(wide_direction * image, axis=0, keepdims=True)
        start_sum(thin, 2 * turn + 1, 0, bend)
        final = turn + 1 == ITERS
        if not final:
            flat[...] = image
            halo = (
                wide_own.at[turn], wide_near.at[turn],
                halo_send.at[2 * turn + 1], halo_recv.at[2 * turn + 1],
            )
            for face in range(FACES):
                wide_own[turn, face] = flat[rows_of(face), :]
                send_face(face, *halo)
        step_size = rho / finish_sum(thin, 2 * turn + 1)
        for face in range(FACES):
            move = step_size * direction[face]
            out[face] = move if turn == 0 else out[face] + move
            if not final:
                wait_face(face, *halo)
                joined = wide_own[turn, face] + wide_near[turn, face]
                residual[face] = jnp.where(live[face], residual[face] - step_size * joined, 0.0)
    for turn in range(ITERS):
        drain_sum(wide_sums.at[turn], 2 * turn)
        drain_sum(thin_sums.at[turn], 2 * turn + 1)


def vmem(count):
    return [pl.BlockSpec(memory_space=pltpu.VMEM)] * count


def params(collective_id=None):
    if collective_id is None:
        return pltpu.CompilerParams(vmem_limit_bytes=VMEM_BYTES)
    return pltpu.CompilerParams(
        vmem_limit_bytes=VMEM_BYTES, collective_id=collective_id, has_side_effects=True
    )


def local(local_schur, schur_inverse, load_terms, corner_basis, corner_map, coarse_inverse):
    size, cases = load_terms.shape[4:]
    order = FACES * size
    matrix = local_schur.reshape(order, order)
    inverse = schur_inverse.reshape(order, order)
    load = load_terms.reshape(FACES, size, cases)
    places = [lax.axis_index(axis) for axis in AXES]
    counts = [lax.axis_size(axis) for axis in AXES]
    corners = coarse_inverse.shape[0]
    wide_rows = (corners + 1 + 15) // 16 * 16
    own_corners = corner_map[places[0], places[1], places[2]]
    own_corners = jnp.where(own_corners < corners, own_corners, -1)
    hot = (lax.broadcasted_iota(jnp.int32, (wide_rows, 8), 0) == own_corners[None, :]).astype(jnp.float32)
    basis = corner_basis.reshape(8, FACES, size).transpose(1, 0, 2)
    coarse = jnp.pad(coarse_inverse, ((0, wide_rows - corners), (0, wide_rows - corners)))
    flags = []
    for axis in range(3):
        flags.append(places[axis] > 0)
        flags.append(places[axis] < counts[axis] - 1)
    flags = jnp.stack(flags).astype(jnp.int32)

    tall = (size + 15) // 16 * 16
    broad = (size + 127) // 128 * 128
    padded = (size + PANEL - 1) // PANEL * PANEL
    margins = ((0, tall - size), (0, broad - size))
    blocks = jnp.stack(
        [
            jnp.pad(matrix[f * size : (f + 1) * size, f * size : (f + 1) * size], margins)
            for f in range(FACES)
        ]
    )
    tall_load = jnp.pad(load, ((0, 0), (0, tall - size), (0, 0)))
    near_blocks, near_load = pl.pallas_call(
        exchange_kernel,
        out_shape=[
            jax.ShapeDtypeStruct(blocks.shape, blocks.dtype),
            jax.ShapeDtypeStruct(tall_load.shape, tall_load.dtype),
        ],
        in_specs=vmem(2),
        out_specs=vmem(2),
        scratch_shapes=[pltpu.SemaphoreType.DMA((FACES,))] * 4,
        compiler_params=params(0),
        name="exchange",
    )(blocks, tall_load)

    square = jax.ShapeDtypeStruct((FACES, size, size), jnp.bfloat16)
    factors = pl.pallas_call(
        functools.partial(inverse_kernel, size),
        out_shape=[square] * 2
        + [jax.ShapeDtypeStruct((FACES, wide_rows + size, size), jnp.bfloat16)] * 2
        + [
            jax.ShapeDtypeStruct((FACES, wide_rows, size), jnp.float32),
        ],
        in_specs=[pl.BlockSpec(memory_space=pltpu.SMEM)] + vmem(4),
        out_specs=vmem(5),
        scratch_shapes=[pltpu.VMEM((FACES, padded, padded), jnp.float32)],
        compiler_params=params(),
        name="deluxe",
    )(flags, blocks, near_blocks, basis, hot)

    groups = (("gx", "gy"), ("gz",)) if math.prod(counts) <= 32 else (("gx",), ("gy",), ("gz",))
    slots = sum(group_size(group) for group in groups)
    halos = 2 * ITERS - 1
    face_shape = (FACES, size, cases)
    dma = pltpu.SemaphoreType.DMA
    result = pl.pallas_call(
        functools.partial(cg_kernel, groups),
        out_shape=jax.ShapeDtypeStruct(face_shape, jnp.float32),
        in_specs=vmem(10),
        out_specs=vmem(1)[0],
        scratch_shapes=[
            pltpu.VMEM((FACES, wide_rows, size), jnp.float32),
            pltpu.VMEM((ITERS,) + face_shape, jnp.float32),
            pltpu.VMEM((ITERS,) + face_shape, jnp.float32),
            pltpu.VMEM((ITERS - 1,) + face_shape, jnp.float32),
            pltpu.VMEM((ITERS - 1,) + face_shape, jnp.float32),
            pltpu.VMEM(face_shape, jnp.float32),
            pltpu.VMEM(face_shape, jnp.float32),
            pltpu.VMEM((order, cases), jnp.float32),
            pltpu.VMEM((ITERS, slots, wide_rows, cases), jnp.float32),
            pltpu.VMEM((ITERS, slots, 1, cases), jnp.float32),
            dma((halos, FACES)),
            dma((halos, FACES)),
            dma((FACES,)),
            dma((FACES,)),
            dma((2 * ITERS, slots)),
            dma((2 * ITERS, slots)),
        ],
        compiler_params=params(1),
        name="iterate",
    )(matrix, inverse, load, near_load[:, :size], *factors, coarse)
    return result.reshape(1, 1, 1, FACES, size, cases)


def solution(mesh):
    placed = (
        P("gx", "gy", "gz", None, None),
        P("gx", "gy", "gz", None, None),
        P("gx", "gy", "gz", None, None, None),
        P("gx", "gy", "gz", None, None),
        P(),
        P(),
    )
    return jax.shard_map(
        local,
        mesh=mesh,
        in_specs=placed,
        out_specs=P("gx", "gy", "gz", None, None, None),
        check_vma=False,
    )
```
